256 devices in a mesh: expert: 32 (over x, z_lo, core), tensor: 8 (over y, z_hi).
Axes of the slice: x: 4, y: 4, z: 8 (z_hi: 2, z_lo: 4; z = z_hi * 4 + z_lo), core: 2. Of those that a mesh axis runs over, the one named last changes fastest.
Arguments:
- prior_gate_weight: bfloat16 [32, 7168, 2048], P('expert', None, 'tensor'), may hold values from -6 to 6
- left_factor: bfloat16 [32, 7168, 64], P('expert'), may hold values from -6 to 6
- right_factor: bfloat16 [32, 64, 2048], P('expert', None, 'tensor'), may hold values from -0.75 to 0.75
- refit_expert_index: int32 [32], replicated, may hold values from 0 to 255, as said below
- placement: int32 [64], replicated, may hold values from 0 to 255, as said below
Outputs:
- slot_gate: bfloat16 [64, 7168, 2048], P('expert', None, 'tensor')
The draws below stay inside these ranges and needn't reach their ends.
Inputs may be any that keep to these rules, and one draw needn't show every extreme that they name: `refit_expert_index`: 32 distinct routed expert ids. `placement`: every id is one of refit_expert_index; a quarter of the refit experts are hosted by 4 slots, a quarter by 2 and half by 1.
All inputs are finite; a program needn't handle non-finite values.
Results may differ from the reference program's by a relative error of at most 0.001.
Values may be sent and summed in bfloat16 or wider, within the bound.
A program may use at most 64 MiB of HBM per device.

```python
import jax
import jax.numpy as jnp
from jax import lax

MODEL_WIDTH = 7168
EXPERT_HIDDEN = 2048
ROUTED = 256
UPDATE_RANK = 64
REFIT_TOTAL = 32
SLOTS = 64


def shared_layout(key):
    routed_order = jax.random.permutation(jax.random.fold_in(key, 11), ROUTED)
    refit = routed_order[:REFIT_TOTAL].astype(jnp.int32)
    expert_order = jax.random.permutation(jax.random.fold_in(key, 12), REFIT_TOTAL)
    pattern = jnp.array([4, 1, 1, 2], jnp.int32)
    copies = jnp.zeros((REFIT_TOTAL,), jnp.int32).at[expert_order].set(pattern[jnp.arange(REFIT_TOTAL) % 4])
    owner = jnp.repeat(jnp.arange(REFIT_TOTAL, dtype=jnp.int32), 4)
    within = jnp.tile(jnp.arange(4, dtype=jnp.int32), REFIT_TOTAL)
    usable = within < copies[owner]
    score = jnp.where(usable, 0, 1) * (4 * REFIT_TOTAL) + jnp.arange(4 * REFIT_TOTAL, dtype=jnp.int32)
    chosen = owner[jnp.argsort(score)[:SLOTS]]
    shuffled = chosen[jax.random.permutation(jax.random.fold_in(key, 13), SLOTS)]
    return (refit, refit[shuffled].astype(jnp.int32))


def draw_refit_expert_index(key, part):
    refit, placed = shared_layout(key)
    return refit


def draw_placement(key, part):
    refit, placed = shared_layout(key)
    return placed


def block_levels(rng, shape, cuts, smallest, high):
    def one(position, parts):
        draws = jax.random.uniform(jax.random.fold_in(jax.random.fold_in(rng, 6), position), (parts,), jnp.float32, smallest / len(cuts), high / len(cuts))
        return jnp.repeat(jnp.exp(draws), shape[position] // parts).reshape((-1,) + (1,) * (len(shape) - position - 1))

    factor_of = one(*cuts[0])
    for cut in cuts[1:]:
        factor_of = factor_of * one(*cut)
    return factor_of


def scatter_about(key, dims, deviation, bound, split=(), kind=jnp.bfloat16):
    loudness = block_levels(key, dims, split, -0.22, 0.18) if split else 1.0
    drawn = jax.random.normal(key, dims, jnp.float32) * deviation * loudness
    return jnp.minimum(jnp.maximum(drawn, -bound), bound).astype(kind)


def setup_inputs(seed: int = 0) -> dict:
    keys = jax.random.split(jax.random.key(seed), 6)
    return {
        "prior_gate_weight": scatter_about(keys[0], (REFIT_TOTAL, MODEL_WIDTH, EXPERT_HIDDEN), 1.0, 6.0, ((0, 32), (2, 8))),
        "left_factor": scatter_about(keys[1], (REFIT_TOTAL, MODEL_WIDTH, UPDATE_RANK), 1.0, 6.0, ((0, 32),)),
        "right_factor": scatter_about(keys[2], (REFIT_TOTAL, UPDATE_RANK, EXPERT_HIDDEN), UPDATE_RANK ** -0.5, 0.75, ((0, 32), (2, 8))),
        "refit_expert_index": draw_refit_expert_index(jax.random.fold_in(keys[5], 71), 0),
        "placement": draw_placement(jax.random.fold_in(keys[5], 71), 0),
    }


update_scale = 0.5


def reference(prior_gate_weight, left_factor, right_factor, refit_expert_index, placement):
    match = placement[:, None] == refit_expert_index[None, :]
    slot_pos = jnp.sum(jnp.where(match, jnp.arange(REFIT_TOTAL, dtype=jnp.int32)[None, :], 0), axis=1).astype(jnp.int32)
    present = jnp.any(match, axis=1)

    def one_slot(items):
        slot_position, alive = items
        gate_weight = prior_gate_weight[slot_position].astype(jnp.float32)
        lowrank_update = jnp.dot(left_factor[slot_position], right_factor[slot_position], preferred_element_type=jnp.float32)
        merged_gate = (gate_weight + update_scale * lowrank_update).astype(jnp.bfloat16)
        return jnp.where(alive, merged_gate, jnp.zeros_like(merged_gate))

    return lax.map(one_slot, (slot_pos, present))
```

```python
import functools

import jax
import jax.numpy as jnp
from jax import lax
from jax.experimental import pallas as pl
from jax.experimental.pallas import tpu as pltpu
from jax.sharding import PartitionSpec as P

SCALE = 0.5
COLUMNS = 4
ROWS = 4
ROW_EXPERTS = 8
ROW_SLOTS = 16
CHUNK = 32
CAPACITIES = (16,)
ZERO = 32
RING = 4
SMEM = pltpu.SMEM
VMEM = pltpu.VMEM
MESH = pl.DeviceIdType.MESH


def position():
    e = lax.axis_index("expert")
    return e // 8, (e // 2) % 4, e % 2


def plan_kernel(refit, placement, table, needed, where, slot_at, want, place):
    _, z, _ = position()
    experts, slots = refit.shape[0], placement.shape[0]
    for s in range(slots):
        where[placement[s]] = experts
    for p in range(experts):
        where[refit[p]] = p
    for k in range(3 * (experts + 1)):
        want[k] = 0
    for s in range(slots):
        row = (s // 4) % 4
        p = where[placement[s]]
        slot_at[s] = p
        want[p] = want[p] | (1 << row)
    counts = [jnp.int32(0)] * 4
    edge = jnp.logical_or(z == 0, z == 3)
    home = lax.select(z < 2, 0, 1)
    end = lax.select(z < 2, 0, 3)
    middle = lax.select(z < 2, 1, 2)
    for k in range(3 * 32):
        table[k] = 0
    for p in range(experts):
        row, lane = (p // 2) % 4, (p // 8) * 2 + p % 2
        half = row // 2
        mask = want[p]
        crosses = ((mask & (12 if half == 0 else 3)) != 0).astype(jnp.int32)
        to_end = [((mask & (1 << e)) != 0).astype(jnp.int32) if row != e else jnp.int32(0) for e in (0, 3)]
        mid_place = counts[half]
        end_place = lax.select(end == 0, counts[2], counts[3])
        here = lax.select(middle == row, lane, lax.select(home == half, 8 + lane, 16 + mid_place))
        mine = jnp.logical_and(crosses == 1, home == half)
        table[lax.select(mine, mid_place, 96)] = here
        goes = lax.select(end == 0, to_end[0], to_end[1])
        table[lax.select(goes == 1, 32 + end_place, 96)] = here
        place[p] = lax.select(z == row, lane, lax.select(edge, 16 + end_place, here))
        counts[half] = counts[half] + crosses
        counts[2] = counts[2] + to_end[0]
        counts[3] = counts[3] + to_end[1]
    place[experts] = ZERO
    for k in range(ROW_SLOTS):
        s = (k // 4) * 16 + z * 4 + k % 4
        table[64 + k] = place[slot_at[s]]
    needed[0] = jnp.maximum(jnp.maximum(counts[0], counts[1]), jnp.maximum(counts[2], counts[3]))


def make_plan(refit, placement):
    return pl.pallas_call(
        plan_kernel,
        out_shape=(jax.ShapeDtypeStruct((128,), jnp.int32), jax.ShapeDtypeStruct((1,), jnp.int32)),
        in_specs=[pl.BlockSpec(memory_space=SMEM)] * 2,
        out_specs=(pl.BlockSpec(memory_space=SMEM),) * 2,
        scratch_shapes=[SMEM((256,), jnp.int32), SMEM((64,), jnp.int32), SMEM((128,), jnp.int32), SMEM((40,), jnp.int32)],
        name="plan",
    )(refit, placement)


def place_kernel(capacity, steps, table, prior, left, right, out, sib, own, row, far, near, mids, ends, pair, final, work,
                 sib_in, row_in, far_in, near_in, pair_in, out_in, sent):
    x, z, c = position()
    t_axis = lax.axis_index("tensor")
    size = CHUNK
    width = prior.shape[2]
    block = prior.shape[1] // COLUMNS
    edge = jnp.logical_or(z == 0, z == 3)
    middle = jnp.logical_not(edge)
    along = lax.select(z < 2, 1 - z, 5 - z)
    across = lax.select(z == 1, 2, 1)

    def at(x_, z_, c_):
        return (x_ * 8 + z_ * 2 + c_, t_axis)

    sibling = at(x, z, 1 - c)
    inward = at(x, along, c)
    other = at(x, lax.select(edge, along, across), c)

    def remote(src, dst, send, recv, to):
        return pltpu.make_async_remote_copy(src_ref=src, dst_ref=dst, send_sem=sent.at[send], recv_sem=recv, device_id=to, device_id_type=MESH)

    def compute(t):
        for g in range(COLUMNS):
            for mine in (True, False):
                half = c if mine else 1 - c
                start = pl.multiple_of(g * block + t * (2 * size) + half * size, size)
                rows = pl.ds(start, size)
                update = jnp.dot(left[0, rows, :], right[0], preferred_element_type=jnp.float32)
                merged = (prior[0, rows, :].astype(jnp.float32) + SCALE * update).astype(jnp.bfloat16)
                if mine:
                    own[t, g, c] = merged
                else:
                    sib[t, g] = merged
        remote(sib.at[t], own.at[t, :, c], 0, sib_in.at[t], sibling).start()

    def scatter(t):
        remote(sib.at[t], own.at[t, :, 1 - c], 0, sib_in.at[t], sibling).wait_recv()
        for d in (2, 1, 3):
            to = (x + d) % COLUMNS
            remote(own.at[t, to], row.at[t, pl.ds(2 * x, 2)], 1, row_in.at[t], at(to, z, c)).start()
        row[t, pl.ds(2 * x, 2)] = own[t, x]

    def row_arrived(t):
        remote(row.at[t, pl.ds(0, 6)], row.at[t, pl.ds(0, 6)], 1, row_in.at[t], sibling).wait_recv()

    def edge_send(t):
        row_arrived(t)
        remote(row.at[t], far.at[t], 2, far_in.at[t], inward).start()

    def pick_mid(t):
        row_arrived(t)
        remote(row.at[t], far.at[t], 2, far_in.at[t], inward).wait_recv()
        w = t % RING
        work[w, 0:8] = row[t]
        work[w, 8:16] = far[t]
        for k in range(capacity):
            mids[t, k] = work[w, table[k]]
        remote(mids.at[t], near.at[t], 3, near_in.at[t], other).start()

    def pick_slots(t):
        w = t % RING
        for k in range(ROW_SLOTS):
            g, core, j = k // 4, (k // 2) % 2, k % 2
            half = c if core == 0 else 1 - c
            piece = work[w, table[64 + g * 4 + half * 2 + j]]
            if core == 0:
                final[t, g, j, pl.ds(pl.multiple_of(c * size, size), size)] = piece
            else:
                pair[t, g, j] = piece
        remote(pair.at[t], final.at[t, :, :, pl.ds(pl.multiple_of(c * size, size), size)], 5, pair_in.at[t], sibling).start()

    def near_arrived(t):
        remote(near.at[t], near.at[t], 3, near_in.at[t], other).wait_recv()
        work[t % RING, 16:16 + capacity] = near[t]

    def finish_middle(t):
        near_arrived(t)
        w = t % RING
        for k in range(capacity):
            ends[t, k] = work[w, table[32 + k]]
        remote(ends.at[t], near.at[t], 4, near_in.at[t], inward).start()
        pick_slots(t)

    def finish_edge(t):
        near_arrived(t)
        work[t % RING, 0:8] = row[t]
        pick_slots(t)

    def deliver(t):
        remote(pair.at[t], pair.at[t], 5, pair_in.at[t], sibling).wait_recv()
        rows = pl.ds(pl.multiple_of(x * block + t * (2 * size), 2 * size), 2 * size)
        for d in (2, 1, 3):
            to = (x + d) % COLUMNS
            remote(final.at[t, to], out.at[:, rows], 6, out_in.at[0], at(to, z, c)).start()
        pltpu.make_async_copy(final.at[t, x], out.at[:, rows], out_in.at[1]).start()

    barrier = pltpu.get_barrier_semaphore()
    for peer in (sibling, inward, at((x + 1) % 4, z, c), at((x + 2) % 4, z, c), at((x + 3) % 4, z, c)):
        pl.semaphore_signal(barrier, inc=1, device_id=peer, device_id_type=MESH)

    @pl.when(middle)
    def _():
        pl.semaphore_signal(barrier, inc=1, device_id=other, device_id_type=MESH)

    for w in range(RING):
        work[w, ZERO] = jnp.zeros((size, width), jnp.bfloat16)
    pl.semaphore_wait(barrier, lax.select(middle, 6, 5))

    def stage(i, delay, body, role=None):
        t = i - delay
        live = jnp.logical_and(t >= 0, t < steps)

        @pl.when(live if role is None else jnp.logical_and(live, role))
        def _():
            body(t)

    last = 8

    @pl.loop(0, steps + last)
    def _(i):
        stage(i, 0, compute)
        stage(i, 1, scatter)
        stage(i, 3, edge_send, edge)
        stage(i, 4, pick_mid, middle)
        stage(i, 5, finish_middle, middle)
        stage(i, 7, finish_edge, edge)
        stage(i, 6, deliver, middle)
        stage(i, 8, deliver, edge)

    remote(sib, sib, 0, sib_in.at[0], sibling).wait_send()
    remote(own.at[:, 0:3], own.at[:, 0:3], 1, sib_in.at[0], sibling).wait_send()

    @pl.when(edge)
    def _():
        remote(row, row, 2, sib_in.at[0], sibling).wait_send()

    @pl.when(middle)
    def _():
        remote(mids, mids, 3, sib_in.at[0], sibling).wait_send()
        remote(ends, ends, 4, sib_in.at[0], sibling).wait_send()

    remote(pair, pair, 5, sib_in.at[0], sibling).wait_send()
    remote(final.at[:, 0:3], final.at[:, 0:3], 6, sib_in.at[0], sibling).wait_send()
    most = out.at[:, pl.ds(0, 3 * block)]
    remote(most, most, 6, out_in.at[0], sibling).wait_recv()
    rest = out.at[:, pl.ds(0, block)]
    pltpu.make_async_copy(rest, rest, out_in.at[1]).wait()


def place(capacity, number, table, prior, left, right):
    _, depth, width = prior.shape
    size = CHUNK
    steps = depth // (ROW_EXPERTS * size)
    dtype = jnp.bfloat16

    def buffer(*shape):
        return VMEM(shape + (width,), dtype)

    vmem = pl.BlockSpec(memory_space=VMEM)
    return pl.pallas_call(
        functools.partial(place_kernel, capacity, steps),
        out_shape=jax.ShapeDtypeStruct((2, depth, width), dtype),
        in_specs=[pl.BlockSpec(memory_space=SMEM), vmem, vmem, vmem],
        out_specs=pl.BlockSpec(memory_space=pl.ANY),
        scratch_shapes=[
            buffer(steps, COLUMNS, size),
            buffer(steps, COLUMNS, 2, size),
            buffer(steps, ROW_EXPERTS, size),
            buffer(steps, ROW_EXPERTS, size),
            buffer(steps, capacity, size),
            buffer(steps, capacity, size),
            buffer(steps, capacity, size),
            buffer(steps, COLUMNS, 2, size),
            buffer(steps, COLUMNS, 2, 2 * size),
            buffer(RING, ZERO + 1, size),
            pltpu.SemaphoreType.DMA((steps,)),
            pltpu.SemaphoreType.DMA((steps,)),
            pltpu.SemaphoreType.DMA((steps,)),
            pltpu.SemaphoreType.DMA((steps,)),
            pltpu.SemaphoreType.DMA((steps,)),
            pltpu.SemaphoreType.DMA((2,)),
            pltpu.SemaphoreType.DMA((7,)),
        ],
        compiler_params=pltpu.CompilerParams(collective_id=number, has_side_effects=True, vmem_limit_bytes=62 << 20),
        name="place%d" % capacity,
    )(table, prior, left, right)


def per_device(prior_gate_weight, left_factor, right_factor, refit_expert_index, placement):
    table, needed = make_plan(refit_expert_index, placement)
    operands = (table, prior_gate_weight, left_factor, right_factor)
    if len(CAPACITIES) == 1:
        return place(CAPACITIES[0], 0, *operands)
    branch = sum((needed[0] > capacity).astype(jnp.int32) for capacity in CAPACITIES[:-1])
    branches = [functools.partial(place, capacity, n) for n, capacity in enumerate(CAPACITIES)]
    return lax.switch(branch, branches, *operands)


def solution(mesh):
    return jax.shard_map(
        per_device,
        mesh=mesh,
        in_specs=(
            P("expert", None, "tensor"),
            P("expert", None, None),
            P("expert", None, "tensor"),
            P(),
            P(),
        ),
        out_specs=P("expert", None, "tensor"),
        check_vma=False,
    )
```

```python
import functools

import jax
import jax.numpy as jnp
from jax import lax
from jax.experimental import pallas as pl
from jax.experimental.pallas import tpu as pltpu
from jax.sharding import PartitionSpec as P

SCALE = 0.5
COLUMNS = 4
ROWS = 4
ROW_EXPERTS = 8
ROW_SLOTS = 16
CHUNK = 32
CAPACITIES = (10, 11, 12, 13, 14, 16)
ZERO = 32
RING = 4
EDGE_SEND = 2
PICK_MID = 3
FINISH_MIDDLE = 4
FINISH_EDGE = 6
LAST = FINISH_EDGE + 1
SMEM = pltpu.SMEM
VMEM = pltpu.VMEM
MESH = pl.DeviceIdType.MESH


def position():
    e = lax.axis_index("expert")
    return e // 8, (e // 2) % 4, e % 2


def plan_kernel(refit, placement, table, needed, where, slot_at, want, place):
    _, z, _ = position()
    experts, slots = refit.shape[0], placement.shape[0]
    for s in range(slots):
        where[placement[s]] = experts
    for p in range(experts):
        where[refit[p]] = p
    for k in range(3 * (experts + 1)):
        want[k] = 0
    for s in range(slots):
        row = (s // 4) % 4
        p = where[placement[s]]
        slot_at[s] = p
        want[p] = want[p] | (1 << row)
    counts = [jnp.int32(0)] * 4
    edge = jnp.logical_or(z == 0, z == 3)
    home = lax.select(z < 2, 0, 1)
    end = lax.select(z < 2, 0, 3)
    middle = lax.select(z < 2, 1, 2)
    for k in range(3 * 32):
        table[k] = 0
    for p in range(experts):
        row, lane = (p // 2) % 4, (p // 8) * 2 + p % 2
        half = row // 2
        mask = want[p]
        crosses = ((mask & (12 if half == 0 else 3)) != 0).astype(jnp.int32)
        to_end = [((mask & (1 << e)) != 0).astype(jnp.int32) if row != e else jnp.int32(0) for e in (0, 3)]
        mid_place = counts[half]
        end_place = lax.select(end == 0, counts[2], counts[3])
        here = lax.select(middle == row, lane, lax.select(home == half, 8 + lane, 16 + mid_place))
        mine = jnp.logical_and(crosses == 1, home == half)
        table[lax.select(mine, mid_place, 96)] = here
        goes = lax.select(end == 0, to_end[0], to_end[1])
        table[lax.select(goes == 1, 32 + end_place, 96)] = here
        place[p] = lax.select(z == row, lane, lax.select(edge, 16 + end_place, here))
        counts[half] = counts[half] + crosses
        counts[2] = counts[2] + to_end[0]
        counts[3] = counts[3] + to_end[1]
    place[experts] = ZERO
    for k in range(ROW_SLOTS):
        s = (k // 4) * 16 + z * 4 + k % 4
        table[64 + k] = place[slot_at[s]]
    needed[0] = jnp.maximum(jnp.maximum(counts[0], counts[1]), jnp.maximum(counts[2], counts[3]))


def make_plan(refit, placement):
    return pl.pallas_call(
        plan_kernel,
        out_shape=(jax.ShapeDtypeStruct((128,), jnp.int32), jax.ShapeDtypeStruct((1,), jnp.int32)),
        in_specs=[pl.BlockSpec(memory_space=SMEM)] * 2,
        out_specs=(pl.BlockSpec(memory_space=SMEM),) * 2,
        scratch_shapes=[SMEM((256,), jnp.int32), SMEM((64,), jnp.int32), SMEM((128,), jnp.int32), SMEM((40,), jnp.int32)],
        name="plan",
    )(refit, placement)


def place_kernel(capacity, steps, table, prior, left, right, out, sib, own, row, far, near, mids, ends, pair, final, work,
                 sib_in, row_in, far_in, near_in, pair_in, out_in, sent):
    x, z, c = position()
    t_axis = lax.axis_index("tensor")
    size = CHUNK
    width = prior.shape[2]
    block = prior.shape[1] // COLUMNS
    edge = jnp.logical_or(z == 0, z == 3)
    middle = jnp.logical_not(edge)
    along = lax.select(z < 2, 1 - z, 5 - z)
    across = lax.select(z == 1, 2, 1)

    def at(x_, z_, c_):
        return (x_ * 8 + z_ * 2 + c_, t_axis)

    sibling = at(x, z, 1 - c)
    inward = at(x, along, c)
    other = at(x, lax.select(edge, along, across), c)

    def remote(src, dst, send, recv, to):
        return pltpu.make_async_remote_copy(src_ref=src, dst_ref=dst, send_sem=sent.at[send], recv_sem=recv, device_id=to, device_id_type=MESH)

    def compute(i):
        for g in range(COLUMNS):
            rows = pl.ds(pl.multiple_of(g * block + i * (4 * size), 4 * size), 4 * size)
            update = lax.dot_general(left[0, :, rows], right[0], (((0,), (0,)), ((), ())), preferred_element_type=jnp.float32)
            merged = (prior[0, rows, :].astype(jnp.float32) + SCALE * update).astype(jnp.bfloat16)
            for n in range(2):
                first, second = (merged[(2 * n + m) * size:(2 * n + m + 1) * size] for m in range(2))
                own[2 * i + n, g, c] = jnp.where(c == 0, first, second)
                sib[2 * i + n, g] = jnp.where(c == 0, second, first)
        for n in range(2):
            t = 2 * i + n
            remote(sib.at[t], own.at[t, :, c], 0, sib_in.at[t], sibling).start()

    def scatter(i):
        for n in range(2):
            t = 2 * i + n
            remote(sib.at[t], own.at[t, :, 1 - c], 0, sib_in.at[t], sibling).wait_recv()
            for d in (2, 1, 3):
                to = (x + d) % COLUMNS
                remote(own.at[t, to], row.at[t, pl.ds(2 * x, 2)], 1, row_in.at[t], at(to, z, c)).start()
            row[t, pl.ds(2 * x, 2)] = own[t, x]

    def row_arrived(t):
        remote(row.at[t, pl.ds(0, 6)], row.at[t, pl.ds(0, 6)], 1, row_in.at[t], sibling).wait_recv()

    def edge_send(t):
        row_arrived(t)
        remote(row.at[t], far.at[t], 2, far_in.at[t], inward).start()

    def pick_mid(t):
        row_arrived(t)
        remote(row.at[t], far.at[t], 2, far_in.at[t], inward).wait_recv()
        w = t % RING
        work[w, 0:8] = row[t]
        work[w, 8:16] = far[t]
        for k in range(capacity):
            mids[t, k] = work[w, table[k]]
        remote(mids.at[t], near.at[t], 3, near_in.at[t], other).start()

    def pick_slots(t):
        w = t % RING
        for k in range(ROW_SLOTS):
            g, core, j = k // 4, (k // 2) % 2, k % 2
            half = c if core == 0 else 1 - c
            piece = work[w, table[64 + g * 4 + half * 2 + j]]
            if core == 0:
                final[t, g, j, pl.ds(pl.multiple_of(c * size, size), size)] = piece
            else:
                pair[t, g, j] = piece
        remote(pair.at[t], final.at[t, :, :, pl.ds(pl.multiple_of(c * size, size), size)], 5, pair_in.at[t], sibling).start()

    def near_arrived(t):
        remote(near.at[t], near.at[t], 3, near_in.at[t], other).wait_recv()
        work[t % RING, 16:16 + capacity] = near[t]

    def finish_middle(t):
        near_arrived(t)
        w = t % RING
        for k in range(capacity):
            ends[t, k] = work[w, table[32 + k]]
        remote(ends.at[t], near.at[t], 4, near_in.at[t], inward).start()
        pick_slots(t)

    def finish_edge(t):
        near_arrived(t)
        work[t % RING, 0:8] = row[t]
        pick_slots(t)

    def deliver(t):
        remote(pair.at[t], pair.at[t], 5, pair_in.at[t], sibling).wait_recv()
        rows = pl.ds(pl.multiple_of(x * block + t * (2 * size), 2 * size), 2 * size)
        for d in (2, 1, 3):
            to = (x + d) % COLUMNS
            remote(final.at[t, to], out.at[:, rows], 6, out_in.at[0], at(to, z, c)).start()
        pltpu.make_async_copy(final.at[t, x], out.at[:, rows], out_in.at[1]).start()

    barrier = pltpu.get_barrier_semaphore()
    for peer in (sibling, inward, at((x + 1) % 4, z, c), at((x + 2) % 4, z, c), at((x + 3) % 4, z, c)):
        pl.semaphore_signal(barrier, inc=1, device_id=peer, device_id_type=MESH)

    @pl.when(middle)
    def _():
        pl.semaphore_signal(barrier, inc=1, device_id=other, device_id_type=MESH)

    for w in range(RING):
        work[w, ZERO] = jnp.zeros((size, width), jnp.bfloat16)
    pl.semaphore_wait(barrier, lax.select(middle, 6, 5))

    def stage(i, delay, count, body, role=None):
        t = i - delay
        live = jnp.logical_and(t >= 0, t < count)

        @pl.when(live if role is None else jnp.logical_and(live, role))
        def _():
            body(t)

    @pl.loop(0, steps + LAST)
    def _(i):
        stage(i, 0, steps // 2, compute)
        stage(i, 1, steps // 2, scatter)
        stage(i, EDGE_SEND, steps, edge_send, edge)
        stage(i, PICK_MID, steps, pick_mid, middle)
        stage(i, FINISH_MIDDLE, steps, finish_middle, middle)
        stage(i, FINISH_EDGE, steps, finish_edge, edge)
        stage(i, FINISH_MIDDLE + 1, steps, deliver, middle)
        stage(i, FINISH_EDGE + 1, steps, deliver, edge)

    remote(sib, sib, 0, sib_in.at[0], sibling).wait_send()
    remote(own.at[:, 0:3], own.at[:, 0:3], 1, sib_in.at[0], sibling).wait_send()

    @pl.when(edge)
    def _():
        remote(row, row, 2, sib_in.at[0], sibling).wait_send()

    @pl.when(middle)
    def _():
        remote(mids, mids, 3, sib_in.at[0], sibling).wait_send()
        remote(ends, ends, 4, sib_in.at[0], sibling).wait_send()

    remote(pair, pair, 5, sib_in.at[0], sibling).wait_send()
    remote(final.at[:, 0:3], final.at[:, 0:3], 6, sib_in.at[0], sibling).wait_send()
    most = out.at[:, pl.ds(0, 3 * block)]
    remote(most, most, 6, out_in.at[0], sibling).wait_recv()
    rest = out.at[:, pl.ds(0, block)]
    pltpu.make_async_copy(rest, rest, out_in.at[1]).wait()


def place(capacity, number, table, prior, left, right):
    _, depth, width = prior.shape
    size = CHUNK
    steps = depth // (ROW_EXPERTS * size)
    dtype = jnp.bfloat16

    def buffer(*shape):
        return VMEM(shape + (width,), dtype)

    vmem = pl.BlockSpec(memory_space=VMEM)
    return pl.pallas_call(
        functools.partial(place_kernel, capacity, steps),
        out_shape=jax.ShapeDtypeStruct((2, depth, width), dtype),
        in_specs=[pl.BlockSpec(memory_space=SMEM), vmem, vmem, vmem],
        out_specs=pl.BlockSpec(memory_space=pl.ANY),
        scratch_shapes=[
            buffer(steps, COLUMNS, size),
            buffer(steps, COLUMNS, 2, size),
            buffer(steps, ROW_EXPERTS, size),
            buffer(steps, ROW_EXPERTS, size),
            buffer(steps, capacity, size),
            buffer(steps, capacity, size),
            buffer(steps, capacity, size),
            buffer(steps, COLUMNS, 2, size),
            buffer(steps, COLUMNS, 2, 2 * size),
            buffer(RING, ZERO + 1, size),
            pltpu.SemaphoreType.DMA((steps,)),
            pltpu.SemaphoreType.DMA((steps,)),
            pltpu.SemaphoreType.DMA((steps,)),
            pltpu.SemaphoreType.DMA((steps,)),
            pltpu.SemaphoreType.DMA((steps,)),
            pltpu.SemaphoreType.DMA((2,)),
            pltpu.SemaphoreType.DMA((7,)),
        ],
        compiler_params=pltpu.CompilerParams(collective_id=number, has_side_effects=True, vmem_limit_bytes=62 << 20),
        name="place%d" % capacity,
    )(table, prior, left, right)


def per_device(prior_gate_weight, left_factor, right_factor, refit_expert_index, placement):
    table, needed = make_plan(refit_expert_index, placement)
    operands = (table, prior_gate_weight, jnp.swapaxes(left_factor, 1, 2), right_factor)
    if len(CAPACITIES) == 1:
        return place(CAPACITIES[0], 0, *operands)
    branch = sum((needed[0] > capacity).astype(jnp.int32) for capacity in CAPACITIES[:-1])
    branches = [functools.partial(place, capacity, n) for n, capacity in enumerate(CAPACITIES)]
    return lax.switch(branch, branches, *operands)


def solution(mesh):
    return jax.shard_map(
        per_device,
        mesh=mesh,
        in_specs=(
            P("expert", None, "tensor"),
            P("expert", None, None),
            P("expert", None, "tensor"),
            P(),
            P(),
        ),
        out_specs=P("expert", None, "tensor"),
        check_vma=False,
    )
```

```python
import functools

import jax
import jax.numpy as jnp
from jax import lax
from jax.experimental import pallas as pl
from jax.experimental.pallas import tpu as pltpu
from jax.sharding import PartitionSpec as P

SCALE = 0.5
COLUMNS = 4
ROWS = 4
ROW_EXPERTS = 8
ROW_SLOTS = 16
CHUNK = 16
CAPACITIES = (10, 11, 12, 13, 14, 16)
ZERO = 32
RING = 8
GROUP = 8
EDGE_SEND = 2
PICK_MID = 4
FINISH_MIDDLE = 8
FINISH_EDGE = 12
LAST = FINISH_EDGE + 1
SMEM = pltpu.SMEM
VMEM = pltpu.VMEM
MESH = pl.DeviceIdType.MESH


def position():
    e = lax.axis_index("expert")
    return e // 8, (e // 2) % 4, e % 2


def plan_kernel(refit, placement, table, needed, where, slot_at, want, place):
    _, z, _ = position()
    experts, slots = refit.shape[0], placement.shape[0]
    for s in range(slots):
        where[placement[s]] = experts
    for p in range(experts):
        where[refit[p]] = p
    for k in range(3 * (experts + 1)):
        want[k] = 0
    for s in range(slots):
        row = (s // 4) % 4
        p = where[placement[s]]
        slot_at[s] = p
        want[p] = want[p] | (1 << row)
    counts = [jnp.int32(0)] * 4
    edge = jnp.logical_or(z == 0, z == 3)
    home = lax.select(z < 2, 0, 1)
    end = lax.select(z < 2, 0, 3)
    middle = lax.select(z < 2, 1, 2)
    for k in range(3 * 32):
        table[k] = 0
    for p in range(experts):
        row, lane = (p // 2) % 4, (p // 8) * 2 + p % 2
        half = row // 2
        mask = want[p]
        crosses = ((mask & (12 if half == 0 else 3)) != 0).astype(jnp.int32)
        to_end = [((mask & (1 << e)) != 0).astype(jnp.int32) if row != e else jnp.int32(0) for e in (0, 3)]
        mid_place = counts[half]
        end_place = lax.select(end == 0, counts[2], counts[3])
        here = lax.select(middle == row, lane, lax.select(home == half, 8 + lane, 16 + mid_place))
        mine = jnp.logical_and(crosses == 1, home == half)
        table[lax.select(mine, mid_place, 96)] = here
        goes = lax.select(end == 0, to_end[0], to_end[1])
        table[lax.select(goes == 1, 32 + end_place, 96)] = here
        place[p] = lax.select(z == row, lane, lax.select(edge, 16 + end_place, here))
        counts[half] = counts[half] + crosses
        counts[2] = counts[2] + to_end[0]
        counts[3] = counts[3] + to_end[1]
    place[experts] = ZERO
    for k in range(ROW_SLOTS):
        s = (k // 4) * 16 + z * 4 + k % 4
        table[64 + k] = place[slot_at[s]]
    needed[0] = jnp.maximum(jnp.maximum(counts[0], counts[1]), jnp.maximum(counts[2], counts[3]))


def make_plan(refit, placement):
    return pl.pallas_call(
        plan_kernel,
        out_shape=(jax.ShapeDtypeStruct((128,), jnp.int32), jax.ShapeDtypeStruct((1,), jnp.int32)),
        in_specs=[pl.BlockSpec(memory_space=SMEM)] * 2,
        out_specs=(pl.BlockSpec(memory_space=SMEM),) * 2,
        scratch_shapes=[SMEM((256,), jnp.int32), SMEM((64,), jnp.int32), SMEM((128,), jnp.int32), SMEM((40,), jnp.int32)],
        name="plan",
    )(refit, placement)


def place_kernel(capacity, steps, table, prior, left, right, out, sib, own, row, far, near, mids, ends, pair, final, work,
                 sib_in, row_in, far_in, near_in, pair_in, out_in, sent):
    x, z, c = position()
    t_axis = lax.axis_index("tensor")
    size = CHUNK
    front = 128 // (2 * size)
    width = prior.shape[2]
    block = prior.shape[1] // COLUMNS
    edge = jnp.logical_or(z == 0, z == 3)
    middle = jnp.logical_not(edge)
    along = lax.select(z < 2, 1 - z, 5 - z)
    across = lax.select(z == 1, 2, 1)

    def at(x_, z_, c_):
        return (x_ * 8 + z_ * 2 + c_, t_axis)

    sibling = at(x, z, 1 - c)
    inward = at(x, along, c)
    other = at(x, lax.select(edge, along, across), c)

    def remote(src, dst, send, recv, to):
        return pltpu.make_async_remote_copy(src_ref=src, dst_ref=dst, send_sem=sent.at[send], recv_sem=recv, device_id=to, device_id_type=MESH)

    def compute(i):
        for g in range(COLUMNS):
            rows = pl.ds(pl.multiple_of(g * block + i * 128, 128), 128)
            update = lax.dot_general(left[0, :, rows], right[0], (((0,), (0,)), ((), ())), preferred_element_type=jnp.float32)
            merged = (prior[0, rows, :].astype(jnp.float32) + SCALE * update).astype(jnp.bfloat16)
            for n in range(front):
                first, second = (merged[(2 * n + m) * size:(2 * n + m + 1) * size] for m in range(2))
                own[front * i + n, g, c] = jnp.where(c == 0, first, second)
                sib[front * i + n, g] = jnp.where(c == 0, second, first)
        for n in range(front):
            t = front * i + n
            remote(sib.at[t], own.at[t, :, c], 0, sib_in.at[t], sibling).start()

    def scatter(i):
        for n in range(front):
            t = front * i + n
            remote(sib.at[t], own.at[t, :, 1 - c], 0, sib_in.at[t], sibling).wait_recv()
            for d in (2, 1, 3):
                to = (x + d) % COLUMNS
                remote(own.at[t, to], row.at[t, pl.ds(2 * x, 2)], 1, row_in.at[t], at(to, z, c)).start()
            row[t, pl.ds(2 * x, 2)] = own[t, x]

    def row_arrived(t):
        remote(row.at[t, pl.ds(0, 6)], row.at[t, pl.ds(0, 6)], 1, row_in.at[t], sibling).wait_recv()

    def edge_send(t):
        row_arrived(t)
        remote(row.at[t], far.at[t], 2, far_in.at[t], inward).start()

    def pick(w, to, t, start):
        for low in range(0, capacity, GROUP):
            spots = range(low, min(low + GROUP, capacity))
            pieces = [work[w, table[start + k]] for k in spots]
            for k, piece in zip(spots, pieces):
                to[t, k] = piece

    def pick_mid(t):
        row_arrived(t)
        remote(row.at[t], far.at[t], 2, far_in.at[t], inward).wait_recv()
        w = t % RING
        work[w, 0:8] = row[t]
        work[w, 8:16] = far[t]
        pick(w, mids, t, 0)
        remote(mids.at[t], near.at[t], 3, near_in.at[t], other).start()

    def pick_slots(t):
        w = t % RING
        mine = pl.ds(pl.multiple_of(c * size, size), size)
        for core in range(2):
            half = c if core == 0 else 1 - c
            for low in range(0, COLUMNS, GROUP // 2):
                spots = [(g, j) for g in range(low, min(low + GROUP // 2, COLUMNS)) for j in range(2)]
                pieces = [work[w, table[64 + g * 4 + half * 2 + j]] for g, j in spots]
                for (g, j), piece in zip(spots, pieces):
                    if core == 0:
                        final[t, g, j, mine] = piece
                    else:
                        pair[t, g, j] = piece
        remote(pair.at[t], final.at[t, :, :, mine], 5, pair_in.at[t], sibling).start()

    def near_arrived(t):
        remote(near.at[t], near.at[t], 3, near_in.at[t], other).wait_recv()
        work[t % RING, 16:16 + capacity] = near[t]

    def finish_middle(t):
        near_arrived(t)
        w = t % RING
        pick(w, ends, t, 32)
        remote(ends.at[t], near.at[t], 4, near_in.at[t], inward).start()
        pick_slots(t)

    def finish_edge(t):
        near_arrived(t)
        work[t % RING, 0:8] = row[t]
        pick_slots(t)

    def deliver(t):
        remote(pair.at[t], pair.at[t], 5, pair_in.at[t], sibling).wait_recv()
        rows = pl.ds(pl.multiple_of(x * block + t * (2 * size), 2 * size), 2 * size)
        for d in (2, 1, 3):
            to = (x + d) % COLUMNS
            remote(final.at[t, to], out.at[:, rows], 6, out_in.at[0], at(to, z, c)).start()
        pltpu.make_async_copy(final.at[t, x], out.at[:, rows], out_in.at[1]).start()

    barrier = pltpu.get_barrier_semaphore()
    for peer in (sibling, inward, at((x + 1) % 4, z, c), at((x + 2) % 4, z, c), at((x + 3) % 4, z, c)):
        pl.semaphore_signal(barrier, inc=1, device_id=peer, device_id_type=MESH)

    @pl.when(middle)
    def _():
        pl.semaphore_signal(barrier, inc=1, device_id=other, device_id_type=MESH)

    for w in range(RING):
        work[w, ZERO] = jnp.zeros((size, width), jnp.bfloat16)
    pl.semaphore_wait(barrier, lax.select(middle, 6, 5))

    def stage(i, delay, count, body, role=None):
        t = i - delay
        live = jnp.logical_and(t >= 0, t < count)

        @pl.when(live if role is None else jnp.logical_and(live, role))
        def _():
            body(t)

    @pl.loop(0, steps + LAST)
    def _(i):
        stage(i, 0, steps // front, compute)
        stage(i, 1, steps // front, scatter)
        stage(i, EDGE_SEND, steps, edge_send, edge)
        stage(i, PICK_MID, steps, pick_mid, middle)
        stage(i, FINISH_MIDDLE, steps, finish_middle, middle)
        stage(i, FINISH_EDGE, steps, finish_edge, edge)
        stage(i, FINISH_MIDDLE + 1, steps, deliver, middle)
        stage(i, FINISH_EDGE + 1, steps, deliver, edge)

    remote(sib, sib, 0, sib_in.at[0], sibling).wait_send()
    remote(own.at[:, 0:3], own.at[:, 0:3], 1, sib_in.at[0], sibling).wait_send()

    @pl.when(edge)
    def _():
        remote(row, row, 2, sib_in.at[0], sibling).wait_send()

    @pl.when(middle)
    def _():
        remote(mids, mids, 3, sib_in.at[0], sibling).wait_send()
        remote(ends, ends, 4, sib_in.at[0], sibling).wait_send()

    remote(pair, pair, 5, sib_in.at[0], sibling).wait_send()
    remote(final.at[:, 0:3], final.at[:, 0:3], 6, sib_in.at[0], sibling).wait_send()
    most = out.at[:, pl.ds(0, 3 * block)]
    remote(most, most, 6, out_in.at[0], sibling).wait_recv()
    rest = out.at[:, pl.ds(0, block)]
    pltpu.make_async_copy(rest, rest, out_in.at[1]).wait()


def place(capacity, number, table, prior, left, right):
    _, depth, width = prior.shape
    size = CHUNK
    steps = depth // (ROW_EXPERTS * size)
    dtype = jnp.bfloat16

    def buffer(*shape):
        return VMEM(shape + (width,), dtype)

    vmem = pl.BlockSpec(memory_space=VMEM)
    return pl.pallas_call(
        functools.partial(place_kernel, capacity, steps),
        out_shape=VMEM((2, depth, width), dtype),
        in_specs=[pl.BlockSpec(memory_space=SMEM), vmem, vmem, vmem],
        out_specs=vmem,
        scratch_shapes=[
            buffer(steps, COLUMNS, size),
            buffer(steps, COLUMNS, 2, size),
            buffer(steps, ROW_EXPERTS, size),
            buffer(steps, ROW_EXPERTS, size),
            buffer(steps, capacity, size),
            buffer(steps, capacity, size),
            buffer(steps, capacity, size),
            buffer(steps, COLUMNS, 2, size),
            buffer(steps, COLUMNS, 2, 2 * size),
            buffer(RING, ZERO + 1, size),
            pltpu.SemaphoreType.DMA((steps,)),
            pltpu.SemaphoreType.DMA((steps,)),
            pltpu.SemaphoreType.DMA((steps,)),
            pltpu.SemaphoreType.DMA((steps,)),
            pltpu.SemaphoreType.DMA((steps,)),
            pltpu.SemaphoreType.DMA((2,)),
            pltpu.SemaphoreType.DMA((7,)),
        ],
        compiler_params=pltpu.CompilerParams(collective_id=number, has_side_effects=True, vmem_limit_bytes=52 << 20),
        name="place%d" % capacity,
    )(table, prior, left, right)


def per_device(prior_gate_weight, left_factor, right_factor, refit_expert_index, placement):
    table, needed = make_plan(refit_expert_index, placement)
    operands = (table, prior_gate_weight, jnp.swapaxes(left_factor, 1, 2), right_factor)
    if len(CAPACITIES) == 1:
        return place(CAPACITIES[0], 0, *operands)
    branch = sum((needed[0] > capacity).astype(jnp.int32) for capacity in CAPACITIES[:-1])
    branches = [functools.partial(place, capacity, n) for n, capacity in enumerate(CAPACITIES)]
    return lax.switch(branch, branches, *operands)


def solution(mesh):
    return jax.shard_map(
        per_device,
        mesh=mesh,
        in_specs=(
            P("expert", None, "tensor"),
            P("expert", None, None),
            P("expert", None, "tensor"),
            P(),
            P(),
        ),
        out_specs=P("expert", None, "tensor"),
        check_vma=False,
    )
```

```python
import functools

import jax
import jax.numpy as jnp
from jax import lax
from jax.experimental import pallas as pl
from jax.experimental.pallas import tpu as pltpu
from jax.sharding import PartitionSpec as P

SCALE = 0.5
COLUMNS = 4
ROWS = 4
ROW_EXPERTS = 8
ROW_SLOTS = 16
CHUNK = 16
CAPACITIES = (10, 11, 12, 13, 14, 16)
ZERO = 32
RING = 8
GROUP = 8
EDGE_SEND = 3
PICK_MID = 4
FINISH_MIDDLE = 7
FINISH_EDGE = 10
LAST = FINISH_EDGE + 1
SMEM = pltpu.SMEM
VMEM = pltpu.VMEM
MESH = pl.DeviceIdType.MESH


def position():
    e = lax.axis_index("expert")
    return e // 8, (e // 2) % 4, e % 2


def plan_kernel(refit, placement, table, branch, where, slot_at, want, place):
    _, z, _ = position()
    experts, slots = refit.shape[0], placement.shape[0]
    for s in range(slots):
        where[placement[s]] = experts
    for p in range(experts):
        where[refit[p]] = p
    for k in range(3 * (experts + 1)):
        want[k] = 0
    for s in range(slots):
        row = (s // 4) % 4
        p = where[placement[s]]
        slot_at[s] = p
        want[p] = want[p] | (1 << row)
    counts = [jnp.int32(0)] * 4
    edge = jnp.logical_or(z == 0, z == 3)
    home = lax.select(z < 2, 0, 1)
    end = lax.select(z < 2, 0, 3)
    middle = lax.select(z < 2, 1, 2)
    for k in range(3 * 32):
        table[k] = 0
    for p in range(experts):
        row, lane = (p // 2) % 4, (p // 8) * 2 + p % 2
        half = row // 2
        mask = want[p]
        crosses = ((mask & (12 if half == 0 else 3)) != 0).astype(jnp.int32)
        to_end = [((mask & (1 << e)) != 0).astype(jnp.int32) if row != e else jnp.int32(0) for e in (0, 3)]
        mid_place = counts[half]
        end_place = lax.select(end == 0, counts[2], counts[3])
        here = lax.select(middle == row, lane, lax.select(home == half, 8 + lane, 16 + mid_place))
        mine = jnp.logical_and(crosses == 1, home == half)
        table[lax.select(mine, mid_place, 96)] = here
        goes = lax.select(end == 0, to_end[0], to_end[1])
        table[lax.select(goes == 1, 32 + end_place, 96)] = here
        place[p] = lax.select(z == row, lane, lax.select(edge, 16 + end_place, here))
        counts[half] = counts[half] + crosses
        counts[2] = counts[2] + to_end[0]
        counts[3] = counts[3] + to_end[1]
    place[experts] = ZERO
    for k in range(ROW_SLOTS):
        s = (k // 4) * 16 + z * 4 + k % 4
        table[64 + k] = place[slot_at[s]]
    most = jnp.maximum(jnp.maximum(counts[0], counts[1]), jnp.maximum(counts[2], counts[3]))
    branch[0] = sum((most > capacity).astype(jnp.int32) for capacity in CAPACITIES[:-1]) + jnp.int32(0)


def make_plan(refit, placement):
    return pl.pallas_call(
        plan_kernel,
        out_shape=(jax.ShapeDtypeStruct((128,), jnp.int32), jax.ShapeDtypeStruct((1,), jnp.int32)),
        in_specs=[pl.BlockSpec(memory_space=SMEM)] * 2,
        out_specs=(pl.BlockSpec(memory_space=SMEM),) * 2,
        scratch_shapes=[SMEM((256,), jnp.int32), SMEM((64,), jnp.int32), SMEM((128,), jnp.int32), SMEM((40,), jnp.int32)],
        name="plan",
    )(refit, placement)


def place_kernel(capacity, steps, table, prior_all, left_all, right_all, out, prior, left, right, sib, own, row, far, near, mids, ends, pair, final, work,
                 sib_in, row_in, far_in, near_in, pair_in, out_in, sent, fetched):
    x, z, c = position()
    t_axis = lax.axis_index("tensor")
    size = CHUNK
    front = 128 // (2 * size)
    width = prior.shape[2]
    block = prior.shape[1]
    edge = jnp.logical_or(z == 0, z == 3)
    middle = jnp.logical_not(edge)
    along = lax.select(z < 2, 1 - z, 5 - z)
    across = lax.select(z == 1, 2, 1)

    def at(x_, z_, c_):
        return (x_ * 8 + z_ * 2 + c_, t_axis)

    sibling = at(x, z, 1 - c)
    inward = at(x, along, c)
    other = at(x, lax.select(edge, along, across), c)

    def remote(src, dst, send, recv, to):
        return pltpu.make_async_remote_copy(src_ref=src, dst_ref=dst, send_sem=sent.at[send], recv_sem=recv, device_id=to, device_id_type=MESH)

    def compute(i):
        part = i // 2
        for k in range(COLUMNS // 2):
            g = (i % 2) * (COLUMNS // 2) + k
            start = part * 128
            rows = pl.ds(pl.multiple_of(g * block + start, 128), 128)
            update = lax.dot_general(left[0, :, rows], right[0], (((0,), (0,)), ((), ())), preferred_element_type=jnp.float32)
            merged = (prior[g, pl.ds(pl.multiple_of(start, 128), 128), :].astype(jnp.float32) + SCALE * update).astype(jnp.bfloat16)
            for n in range(front):
                first, second = (merged[(2 * n + m) * size:(2 * n + m + 1) * size] for m in range(2))
                own[front * part + n, g, c] = jnp.where(c == 0, first, second)
                sib[front * part + n, g] = jnp.where(c == 0, second, first)

        @pl.when(i % 2 == 1)
        def _():
            for n in range(front):
                t = front * part + n
                remote(sib.at[t], own.at[t, :, c], 0, sib_in.at[t], sibling).start()

    def scatter(i):
        for n in range(front // 2):
            t = front // 2 * i + n
            remote(sib.at[t], own.at[t, :, 1 - c], 0, sib_in.at[t], sibling).wait_recv()
            for d in (2, 1, 3):
                to = (x + d) % COLUMNS
                remote(own.at[t, to], row.at[t, pl.ds(2 * x, 2)], 1, row_in.at[t], at(to, z, c)).start()
            row[t, pl.ds(2 * x, 2)] = own[t, x]

    def row_arrived(t):
        remote(row.at[t, pl.ds(0, 6)], row.at[t, pl.ds(0, 6)], 1, row_in.at[t], sibling).wait_recv()

    def edge_send(t):
        row_arrived(t)
        remote(row.at[t], far.at[t], 2, far_in.at[t], inward).start()

    def pick(w, to, t, start):
        for low in range(0, capacity, GROUP):
            spots = range(low, min(low + GROUP, capacity))
            pieces = [work[w, table[start + k]] for k in spots]
            for k, piece in zip(spots, pieces):
                to[t, k] = piece

    def pick_mid(t):
        row_arrived(t)
        remote(row.at[t], far.at[t], 2, far_in.at[t], inward).wait_recv()
        w = t % RING
        work[w, 0:8] = row[t]
        work[w, 8:16] = far[t]
        pick(w, mids, t, 0)
        remote(mids.at[t], near.at[t], 3, near_in.at[t], other).start()

    def pick_slots(t):
        w = t % RING
        mine = pl.ds(pl.multiple_of(c * size, size), size)
        for core in range(2):
            half = c if core == 0 else 1 - c
            for low in range(0, COLUMNS, GROUP // 2):
                spots = [(g, j) for g in range(low, min(low + GROUP // 2, COLUMNS)) for j in range(2)]
                pieces = [work[w, table[64 + g * 4 + half * 2 + j]] for g, j in spots]
                for (g, j), piece in zip(spots, pieces):
                    if core == 0:
                        final[t, g, j, mine] = piece
                    else:
                        pair[t, g, j] = piece
        remote(pair.at[t], final.at[t, :, :, mine], 5, pair_in.at[t], sibling).start()

    def near_arrived(t):
        remote(near.at[t], near.at[t], 3, near_in.at[t], other).wait_recv()
        work[t % RING, 16:16 + capacity] = near[t]

    def finish_middle(t):
        near_arrived(t)
        w = t % RING
        pick(w, ends, t, 32)
        remote(ends.at[t], near.at[t], 4, near_in.at[t], inward).start()
        pick_slots(t)

    def finish_edge(t):
        near_arrived(t)
        work[t % RING, 0:8] = row[t]
        pick_slots(t)

    def deliver(t):
        remote(pair.at[t], pair.at[t], 5, pair_in.at[t], sibling).wait_recv()
        rows = pl.ds(pl.multiple_of(x * block + t * (2 * size), 2 * size), 2 * size)
        for d in (2, 1, 3):
            to = (x + d) % COLUMNS
            remote(final.at[t, to], out.at[:, rows], 6, out_in.at[0], at(to, z, c)).start()
        pltpu.make_async_copy(final.at[t, x], out.at[:, rows], out_in.at[1]).start()

    early, late = pl.ds(0, 128), pl.ds(128, block - 128)
    fetches = [
        pltpu.make_async_copy(right_all, right, fetched.at[0]),
        pltpu.make_async_copy(prior_all.at[:, early], prior.at[:, early], fetched.at[1]),
        pltpu.make_async_copy(left_all, left, fetched.at[2]),
        pltpu.make_async_copy(prior_all.at[:, late], prior.at[:, late], fetched.at[3]),
    ]
    for fetch in fetches:
        fetch.start()
    barrier = pltpu.get_barrier_semaphore()
    for peer in (sibling, inward, at((x + 1) % 4, z, c), at((x + 2) % 4, z, c), at((x + 3) % 4, z, c)):
        pl.semaphore_signal(barrier, inc=1, device_id=peer, device_id_type=MESH)

    @pl.when(middle)
    def _():
        pl.semaphore_signal(barrier, inc=1, device_id=other, device_id_type=MESH)

    for w in range(RING):
        work[w, ZERO] = jnp.zeros((size, width), jnp.bfloat16)
    for fetch in fetches[:3]:
        fetch.wait()
    pl.semaphore_wait(barrier, lax.select(middle, 6, 5))

    def stage(i, delay, count, body, role=None):
        t = i - delay
        live = jnp.logical_and(t >= 0, t < count)

        @pl.when(live if role is None else jnp.logical_and(live, role))
        def _():
            body(t)

    @pl.loop(0, steps + LAST)
    def _(i):
        @pl.when(i == 2)
        def _():
            fetches[3].wait()

        stage(i, 0, 2 * steps // front, compute)
        stage(i, 2, 2 * steps // front, scatter)
        stage(i, EDGE_SEND, steps, edge_send, edge)
        stage(i, PICK_MID, steps, pick_mid, middle)
        stage(i, FINISH_MIDDLE, steps, finish_middle, middle)
        stage(i, FINISH_EDGE, steps, finish_edge, edge)
        stage(i, FINISH_MIDDLE + 1, steps, deliver, middle)
        stage(i, FINISH_EDGE + 1, steps, deliver, edge)

    remote(sib, sib, 0, sib_in.at[0], sibling).wait_send()
    remote(own.at[:, 0:3], own.at[:, 0:3], 1, sib_in.at[0], sibling).wait_send()

    @pl.when(edge)
    def _():
        remote(row, row, 2, sib_in.at[0], sibling).wait_send()

    @pl.when(middle)
    def _():
        remote(mids, mids, 3, sib_in.at[0], sibling).wait_send()
        remote(ends, ends, 4, sib_in.at[0], sibling).wait_send()

    remote(pair, pair, 5, sib_in.at[0], sibling).wait_send()
    remote(final.at[:, 0:3], final.at[:, 0:3], 6, sib_in.at[0], sibling).wait_send()
    most = out.at[:, pl.ds(0, 3 * block)]
    remote(most, most, 6, out_in.at[0], sibling).wait_recv()
    rest = out.at[:, pl.ds(0, block)]
    pltpu.make_async_copy(rest, rest, out_in.at[1]).wait()


def place(capacity, number, table, prior, left, right):
    _, depth, width = prior.shape
    prior = prior.reshape(COLUMNS, depth // COLUMNS, width)
    size = CHUNK
    steps = depth // (ROW_EXPERTS * size)
    dtype = jnp.bfloat16

    def buffer(*shape):
        return VMEM(shape + (width,), dtype)

    vmem = pl.BlockSpec(memory_space=VMEM)
    return pl.pallas_call(
        functools.partial(place_kernel, capacity, steps),
        out_shape=VMEM((2, depth, width), dtype),
        in_specs=[pl.BlockSpec(memory_space=SMEM)] + [pl.BlockSpec(memory_space=pl.ANY)] * 3,
        out_specs=vmem,
        scratch_shapes=[
            VMEM(prior.shape, dtype),
            VMEM(left.shape, dtype),
            VMEM(right.shape, dtype),
            buffer(steps, COLUMNS, size),
            buffer(steps, COLUMNS, 2, size),
            buffer(steps, ROW_EXPERTS, size),
            buffer(steps, ROW_EXPERTS, size),
            buffer(steps, capacity, size),
            buffer(steps, capacity, size),
            buffer(steps, capacity, size),
            buffer(steps, COLUMNS, 2, size),
            buffer(steps, COLUMNS, 2, 2 * size),
            buffer(RING, ZERO + 1, size),
            pltpu.SemaphoreType.DMA((steps,)),
            pltpu.SemaphoreType.DMA((steps,)),
            pltpu.SemaphoreType.DMA((steps,)),
            pltpu.SemaphoreType.DMA((steps,)),
            pltpu.SemaphoreType.DMA((steps,)),
            pltpu.SemaphoreType.DMA((2,)),
            pltpu.SemaphoreType.DMA((7,)),
            pltpu.SemaphoreType.DMA((4,)),
        ],
        compiler_params=pltpu.CompilerParams(collective_id=number, has_side_effects=True, vmem_limit_bytes=52 << 20),
        name="place%d" % capacity,
    )(table, prior, left, right)


def per_device(prior_gate_weight, left_factor, right_factor, refit_expert_index, placement):
    table, branch = make_plan(refit_expert_index, placement)
    operands = (table, prior_gate_weight, jnp.swapaxes(left_factor, 1, 2), right_factor)
    if len(CAPACITIES) == 1:
        return place(CAPACITIES[0], 0, *operands)
    branches = [functools.partial(place, capacity, n) for n, capacity in enumerate(CAPACITIES)]
    return lax.switch(branch[0], branches, *operands)


def solution(mesh):
    return jax.shard_map(
        per_device,
        mesh=mesh,
        in_specs=(
            P("expert", None, "tensor"),
            P("expert", None, None),
            P("expert", None, "tensor"),
            P(),
            P(),
        ),
        out_specs=P("expert", None, "tensor"),
        check_vma=False,
    )
```

```python
import functools

import jax
import jax.numpy as jnp
from jax import lax
from jax.experimental import pallas as pl
from jax.experimental.pallas import tpu as pltpu
from jax.sharding import PartitionSpec as P

SCALE = 0.5
COLUMNS = 4
ROWS = 4
ROW_EXPERTS = 8
ROW_SLOTS = 16
CHUNK = 16
CAPACITIES = (10, 11, 12, 13, 14, 16)
ZERO = 32
RING = 8
GROUP = 8
EDGE_SEND = 2
PICK_MID = 3
FINISH_MIDDLE = 6
FINISH_EDGE = 9
LAST = FINISH_EDGE + 1
SMEM = pltpu.SMEM
VMEM = pltpu.VMEM
MESH = pl.DeviceIdType.MESH


def position():
    e = lax.axis_index("expert")
    return e // 8, (e // 2) % 4, e % 2


def plan_kernel(refit, placement, table, branch, where, slot_at, want, place):
    _, z, _ = position()
    experts, slots = refit.shape[0], placement.shape[0]
    for s in range(slots):
        where[placement[s]] = experts
    for p in range(experts):
        where[refit[p]] = p
    for k in range(3 * (experts + 1)):
        want[k] = 0
    for s in range(slots):
        row = (s // 4) % 4
        p = where[placement[s]]
        slot_at[s] = p
        want[p] = want[p] | (1 << row)
    counts = [jnp.int32(0)] * 4
    edge = jnp.logical_or(z == 0, z == 3)
    home = lax.select(z < 2, 0, 1)
    end = lax.select(z < 2, 0, 3)
    middle = lax.select(z < 2, 1, 2)
    for k in range(3 * 32):
        table[k] = 0
    for p in range(experts):
        row, lane = (p // 2) % 4, (p // 8) * 2 + p % 2
        half = row // 2
        mask = want[p]
        crosses = ((mask & (12 if half == 0 else 3)) != 0).astype(jnp.int32)
        to_end = [((mask & (1 << e)) != 0).astype(jnp.int32) if row != e else jnp.int32(0) for e in (0, 3)]
        mid_place = counts[half]
        end_place = lax.select(end == 0, counts[2], counts[3])
        here = lax.select(middle == row, lane, lax.select(home == half, 8 + lane, 16 + mid_place))
        mine = jnp.logical_and(crosses == 1, home == half)
        table[lax.select(mine, mid_place, 96)] = here
        goes = lax.select(end == 0, to_end[0], to_end[1])
        table[lax.select(goes == 1, 32 + end_place, 96)] = here
        place[p] = lax.select(z == row, lane, lax.select(edge, 16 + end_place, here))
        counts[half] = counts[half] + crosses
        counts[2] = counts[2] + to_end[0]
        counts[3] = counts[3] + to_end[1]
    place[experts] = ZERO
    for k in range(ROW_SLOTS):
        s = (k // 4) * 16 + z * 4 + k % 4
        table[64 + k] = place[slot_at[s]]
    most = jnp.maximum(jnp.maximum(counts[0], counts[1]), jnp.maximum(counts[2], counts[3]))
    branch[0] = sum((most > capacity).astype(jnp.int32) for capacity in CAPACITIES[:-1]) + jnp.int32(0)


def make_plan(refit, placement):
    return pl.pallas_call(
        plan_kernel,
        out_shape=(SMEM((128,), jnp.int32), jax.ShapeDtypeStruct((1,), jnp.int32)),
        in_specs=[pl.BlockSpec(memory_space=SMEM)] * 2,
        out_specs=(pl.BlockSpec(memory_space=SMEM),) * 2,
        scratch_shapes=[SMEM((256,), jnp.int32), SMEM((64,), jnp.int32), SMEM((128,), jnp.int32), SMEM((40,), jnp.int32)],
        name="plan",
    )(refit, placement)


def place_kernel(capacity, steps, table, prior_all, left_all, right_all, out, prior, left, right, sib, own, row, far, near, mids, ends, pair, final, work,
                 sib_in, row_in, far_in, near_in, pair_in, out_in, sent, fetched):
    x, z, c = position()
    t_axis = lax.axis_index("tensor")
    size = CHUNK
    front = 128 // (2 * size)
    width = prior.shape[2]
    block = prior.shape[1]
    edge = jnp.logical_or(z == 0, z == 3)
    middle = jnp.logical_not(edge)
    along = lax.select(z < 2, 1 - z, 5 - z)
    across = lax.select(z == 1, 2, 1)

    def at(x_, z_, c_):
        return (x_ * 8 + z_ * 2 + c_, t_axis)

    sibling = at(x, z, 1 - c)
    inward = at(x, along, c)
    other = at(x, lax.select(edge, along, across), c)

    def remote(src, dst, send, recv, to):
        return pltpu.make_async_remote_copy(src_ref=src, dst_ref=dst, send_sem=sent.at[send], recv_sem=recv, device_id=to, device_id_type=MESH)

    def compute(i):
        part = i // 2
        for k in range(COLUMNS // 2):
            g = (i % 2) * (COLUMNS // 2) + k
            start = part * 128
            rows = pl.ds(pl.multiple_of(g * block + start, 128), 128)
            update = lax.dot_general(left[0, :, rows], right[0], (((0,), (0,)), ((), ())), preferred_element_type=jnp.float32)
            merged = (prior[g, pl.ds(pl.multiple_of(start, 128), 128), :].astype(jnp.float32) + SCALE * update).astype(jnp.bfloat16)
            for n in range(front):
                first, second = (merged[(2 * n + m) * size:(2 * n + m + 1) * size] for m in range(2))
                own[front * part + n, g, c] = jnp.where(c == 0, first, second)
                sib[front * part + n, g] = jnp.where(c == 0, second, first)

    def exchange(part):
        for n in range(front):
            t = front * part + n
            remote(sib.at[t], own.at[t, :, c], 0, sib_in.at[t], sibling).start()

    def compute_ahead(i):
        compute(i + 2)

        @pl.when(i % 2 == 1)
        def _():
            exchange((i + 2) // 2)

    def scatter(i):
        for n in range(front // 2):
            t = front // 2 * i + n
            remote(sib.at[t], own.at[t, :, 1 - c], 0, sib_in.at[t], sibling).wait_recv()
            for d in (2, 1, 3):
                to = (x + d) % COLUMNS
                remote(own.at[t, to], row.at[t, pl.ds(2 * x, 2)], 1, row_in.at[t], at(to, z, c)).start()
            row[t, pl.ds(2 * x, 2)] = own[t, x]

    def row_arrived(t):
        remote(row.at[t, pl.ds(0, 6)], row.at[t, pl.ds(0, 6)], 1, row_in.at[t], sibling).wait_recv()

    def edge_send(t):
        row_arrived(t)
        remote(row.at[t], far.at[t], 2, far_in.at[t], inward).start()

    def pick(w, to, t, start):
        for low in range(0, capacity, GROUP):
            spots = range(low, min(low + GROUP, capacity))
            pieces = [work[w, table[start + k]] for k in spots]
            for k, piece in zip(spots, pieces):
                to[t, k] = piece

    def pick_mid(t):
        row_arrived(t)
        remote(row.at[t], far.at[t], 2, far_in.at[t], inward).wait_recv()
        w = t % RING
        work[w, 0:8] = row[t]
        work[w, 8:16] = far[t]
        pick(w, mids, t, 0)
        remote(mids.at[t], near.at[t], 3, near_in.at[t], other).start()

    def pick_slots(t):
        w = t % RING
        mine = pl.ds(pl.multiple_of(c * size, size), size)
        for core in range(2):
            half = c if core == 0 else 1 - c
            for low in range(0, COLUMNS, GROUP // 2):
                spots = [(g, j) for g in range(low, min(low + GROUP // 2, COLUMNS)) for j in range(2)]
                pieces = [work[w, table[64 + g * 4 + half * 2 + j]] for g, j in spots]
                for (g, j), piece in zip(spots, pieces):
                    if core == 0:
                        final[t, g, j, mine] = piece
                    else:
                        pair[t, g, j] = piece
        remote(pair.at[t], final.at[t, :, :, mine], 5, pair_in.at[t], sibling).start()

    def near_arrived(t):
        remote(near.at[t], near.at[t], 3, near_in.at[t], other).wait_recv()
        work[t % RING, 16:16 + capacity] = near[t]

    def finish_middle(t):
        near_arrived(t)
        w = t % RING
        pick(w, ends, t, 32)
        remote(ends.at[t], near.at[t], 4, near_in.at[t], inward).start()
        pick_slots(t)

    def finish_edge(t):
        near_arrived(t)
        work[t % RING, 0:8] = row[t]
        pick_slots(t)

    def deliver(t):
        remote(pair.at[t], pair.at[t], 5, pair_in.at[t], sibling).wait_recv()
        rows = pl.ds(pl.multiple_of(x * block + t * (2 * size), 2 * size), 2 * size)
        for d in (2, 1, 3):
            to = (x + d) % COLUMNS
            remote(final.at[t, to], out.at[:, rows], 6, out_in.at[0], at(to, z, c)).start()
        pltpu.make_async_copy(final.at[t, x], out.at[:, rows], out_in.at[1]).start()

    early, late = pl.ds(0, 128), pl.ds(128, block - 128)
    fetches = [
        pltpu.make_async_copy(right_all, right, fetched.at[0]),
        pltpu.make_async_copy(prior_all.at[:, early], prior.at[:, early], fetched.at[1]),
        pltpu.make_async_copy(left_all, left, fetched.at[2]),
        pltpu.make_async_copy(prior_all.at[:, late], prior.at[:, late], fetched.at[3]),
    ]
    for fetch in fetches:
        fetch.start()
    barrier = pltpu.get_barrier_semaphore()
    for peer in (sibling, inward, at((x + 1) % 4, z, c), at((x + 2) % 4, z, c), at((x + 3) % 4, z, c)):
        pl.semaphore_signal(barrier, inc=1, device_id=peer, device_id_type=MESH)

    @pl.when(middle)
    def _():
        pl.semaphore_signal(barrier, inc=1, device_id=other, device_id_type=MESH)

    for w in range(RING):
        work[w, ZERO] = jnp.zeros((size, width), jnp.bfloat16)
    for fetch in fetches[:3]:
        fetch.wait()
    compute(0)
    compute(1)
    pl.semaphore_wait(barrier, lax.select(middle, 6, 5))
    exchange(0)
    fetches[3].wait()

    def stage(i, delay, count, body, role=None):
        t = i - delay
        live = jnp.logical_and(t >= 0, t < count)

        @pl.when(live if role is None else jnp.logical_and(live, role))
        def _():
            body(t)

    @pl.loop(0, steps + LAST)
    def _(i):
        stage(i, 0, 2 * steps // front - 2, compute_ahead)
        stage(i, 1, 2 * steps // front, scatter)
        stage(i, EDGE_SEND, steps, edge_send, edge)
        stage(i, PICK_MID, steps, pick_mid, middle)
        stage(i, FINISH_MIDDLE, steps, finish_middle, middle)
        stage(i, FINISH_EDGE, steps, finish_edge, edge)
        stage(i, FINISH_MIDDLE + 1, steps, deliver, middle)
        stage(i, FINISH_EDGE + 1, steps, deliver, edge)

    remote(sib, sib, 0, sib_in.at[0], sibling).wait_send()
    remote(own.at[:, 0:3], own.at[:, 0:3], 1, sib_in.at[0], sibling).wait_send()

    @pl.when(edge)
    def _():
        remote(row, row, 2, sib_in.at[0], sibling).wait_send()

    @pl.when(middle)
    def _():
        remote(mids, mids, 3, sib_in.at[0], sibling).wait_send()
        remote(ends, ends, 4, sib_in.at[0], sibling).wait_send()

    remote(pair, pair, 5, sib_in.at[0], sibling).wait_send()
    remote(final.at[:, 0:3], final.at[:, 0:3], 6, sib_in.at[0], sibling).wait_send()
    most = out.at[:, pl.ds(0, 3 * block)]
    remote(most, most, 6, out_in.at[0], sibling).wait_recv()
    rest = out.at[:, pl.ds(0, block)]
    pltpu.make_async_copy(rest, rest, out_in.at[1]).wait()


def place(capacity, number, table, prior, left, right):
    _, depth, width = prior.shape
    prior = prior.reshape(COLUMNS, depth // COLUMNS, width)
    size = CHUNK
    steps = depth // (ROW_EXPERTS * size)
    dtype = jnp.bfloat16

    def buffer(*shape):
        return VMEM(shape + (width,), dtype)

    vmem = pl.BlockSpec(memory_space=VMEM)
    return pl.pallas_call(
        functools.partial(place_kernel, capacity, steps),
        out_shape=VMEM((2, depth, width), dtype),
        in_specs=[pl.BlockSpec(memory_space=SMEM)] + [pl.BlockSpec(memory_space=pl.ANY)] * 3,
        out_specs=vmem,
        scratch_shapes=[
            VMEM(prior.shape, dtype),
            VMEM(left.shape, dtype),
            VMEM(right.shape, dtype),
            buffer(steps, COLUMNS, size),
            buffer(steps, COLUMNS, 2, size),
            buffer(steps, ROW_EXPERTS, size),
            buffer(steps, ROW_EXPERTS, size),
            buffer(steps, capacity, size),
            buffer(steps, capacity, size),
            buffer(steps, capacity, size),
            buffer(steps, COLUMNS, 2, size),
            buffer(steps, COLUMNS, 2, 2 * size),
            buffer(RING, ZERO + 1, size),
            pltpu.SemaphoreType.DMA((steps,)),
            pltpu.SemaphoreType.DMA((steps,)),
            pltpu.SemaphoreType.DMA((steps,)),
            pltpu.SemaphoreType.DMA((steps,)),
            pltpu.SemaphoreType.DMA((steps,)),
            pltpu.SemaphoreType.DMA((2,)),
            pltpu.SemaphoreType.DMA((7,)),
            pltpu.SemaphoreType.DMA((4,)),
        ],
        compiler_params=pltpu.CompilerParams(collective_id=number, has_side_effects=True, vmem_limit_bytes=52 << 20),
        name="place%d" % capacity,
    )(table, prior, left, right)


def per_device(prior_gate_weight, left_factor, right_factor, refit_expert_index, placement):
    table, branch = make_plan(refit_expert_index, placement)
    operands = (table, prior_gate_weight, jnp.swapaxes(left_factor, 1, 2), right_factor)
    if len(CAPACITIES) == 1:
        return place(CAPACITIES[0], 0, *operands)
    branches = [functools.partial(place, capacity, n) for n, capacity in enumerate(CAPACITIES)]
    return lax.switch(branch[0], branches, *operands)


def solution(mesh):
    return jax.shard_map(
        per_device,
        mesh=mesh,
        in_specs=(
            P("expert", None, "tensor"),
            P("expert", None, None),
            P("expert", None, "tensor"),
            P(),
            P(),
        ),
        out_specs=P("expert", None, "tensor"),
        check_vma=False,
    )
```
